256 devices in a mesh: step: 32 (over z, x), seq: 8 (over y, core).
Axes of the slice: x: 4, y: 4, z: 8, core: 2. Of those that a mesh axis runs over, the one named last changes fastest.
Arguments:
- trajectory: bfloat16 [64, 1024, 2048], P('step', 'seq'), may hold values from -8 to 8
- initial: bfloat16 [1024, 2048], P('seq'), may hold values from -6 to 6
- step_sizes: float32 [64], P('step'), may hold values from 0.02 to 0.1
- time_index: int32 [64], P('step'), may hold values from 0 to 999, as said below
- plan: float32 [1000], replicated, may hold values from 0.02 to 80
- adaln_weight: bfloat16 [256, 4096], replicated, may hold values from -0.375 to 0.375
- query_weight: bfloat16 [2048, 1024], P('step'), may hold values from -1 to 1
- key_weight: bfloat16 [2048, 1024], P('step'), may hold values from -1 to 1
- value_weight: bfloat16 [2048, 1024], P('step'), may hold values from -0.125 to 0.125
- out_weight: bfloat16 [1024, 2048], P('step'), may hold values from -3 to 3
Outputs:
- updated: float32 [64, 1024, 2048], P('step', 'seq')
The draws below stay inside these ranges and needn't reach their ends.
Inputs may be any that keep to these rules, and one draw needn't show every extreme that they name: `time_index`: strictly decreasing along the steps; the first is 999 and the last 0.
All inputs are finite; a program needn't handle non-finite values.
Results may differ from the reference program's by a relative error of at most 0.0054.
Values may be sent and summed in bfloat16 or wider, within the bound.
No kernel may reach another device: no remote copies, remote signals or barrier semaphores. Data moves between devices by JAX's collectives and lax.ppermute only.
A program may use at most 128 MiB of HBM per device.

```python
import math
import jax
import jax.numpy as jnp
from jax import lax

D = 2048
HEAD_DIM = 64
EMB = 256
NSCHED = 1000
HD = 1024
STEPS = 64
L = 1024


def shared_base(key):
    return jax.random.normal(key, (D, HD), jnp.float32)


def draw_query_weight(key, part):
    base = shared_base(key)
    return jnp.clip(base * D ** (-0.5), -1.0, 1.0).astype(jnp.bfloat16)


def draw_key_weight(key, part):
    key = jax.random.fold_in(key, 5)
    noise = jax.random.normal(key, (D, HD), jnp.float32)
    mixed = noise
    return jnp.clip(mixed * D ** (-0.5), -1.0, 1.0).astype(jnp.bfloat16)


def draw_trajectory(key, part):
    key = jax.random.fold_in(key, 7)
    key_list = jax.random.split(key, 1)
    return jax.random.normal(key_list[0], (STEPS, L, D), jnp.float32).astype(jnp.bfloat16)


def draw_time_index(key, part):
    key = jax.random.fold_in(key, 9)
    inner = jax.random.permutation(key, NSCHED - 2)[:STEPS - 2] + 1
    inner = -jnp.sort(-inner)
    return jnp.concatenate([jnp.array([NSCHED - 1], jnp.int32), inner.astype(jnp.int32), jnp.array([0], jnp.int32)])


def block_levels(stream_key, shape, pieces, low, largest):
    factor_of = 1.0
    for position, parts in pieces:
        heights = jax.random.uniform(jax.random.fold_in(jax.random.fold_in(stream_key, 6), position), (parts,), jnp.float32, low / len(pieces), largest / len(pieces))
        factor_of = factor_of * jnp.repeat(jnp.exp(heights), shape[position] // parts).reshape((-1,) + (1,) * (len(shape) - 1 - position))
    return factor_of


def centred(key, dims, width, reach, shards=(), kind=jnp.bfloat16):
    gain = block_levels(key, dims, shards, -0.22, 0.18) if shards else 1.0
    entries = jax.random.normal(key, dims, jnp.float32) * width * gain
    return jnp.minimum(jnp.maximum(entries, -reach), reach).astype(kind)


def setup_inputs(seed: int = 0) -> dict:
    keys = jax.random.split(jax.random.key(seed), 11)
    return {
        "trajectory": draw_trajectory(jax.random.fold_in(keys[10], 71), 0),
        "initial": centred(keys[1], (L, D), 1.0, 6.0, ((0, 8),)),
        "step_sizes": jnp.clip(jnp.exp(math.log(0.1) - 1.609438 * jax.random.uniform(keys[2], (STEPS,), jnp.float32) ** block_levels(keys[2], (STEPS,), ((0, 32),), -0.2, 0.2)), 0.02, 0.1),
        "time_index": draw_time_index(jax.random.fold_in(keys[10], 71), 0),
        "plan": jnp.clip(jnp.exp(jax.random.uniform(keys[4], (NSCHED,), jnp.float32, math.log(0.02), math.log(80.0))), 0.02, 80.0),
        "adaln_weight": centred(keys[5], (EMB, 2 * D), EMB ** -0.5, 0.375),
        "query_weight": draw_query_weight(jax.random.fold_in(keys[10], 71), 0),
        "key_weight": draw_key_weight(jax.random.fold_in(keys[10], 71), 0),
        "value_weight": centred(keys[8], (D, HD), D ** -0.5, 0.125, ((0, 32),)),
        "out_weight": centred(keys[9], (HD, D), (max(HD // 256, 1)) ** -0.5, 3.0, ((0, 32),)),
    }


EPS = 1e-06

def modulation(time_index, plan, adaln_weight):
    sigmas = jnp.take(plan, time_index)
    half_width = adaln_weight.shape[0] // 2
    frequency = 0.25 * jnp.exp(4.0 * jnp.arange(half_width, dtype=jnp.float32) / half_width)
    angles = jnp.log(sigmas)[:, None] * frequency[None, :]
    embedding = jnp.concatenate([jnp.cos(angles), jnp.sin(angles)], axis=1).astype(jnp.bfloat16)
    modulated = jnp.dot(embedding, adaln_weight, preferred_element_type=jnp.float32)
    feature_width = adaln_weight.shape[1] // 2
    return (modulated[:, :feature_width], modulated[:, feature_width:])

def normalize(states, shifts, scales):
    floats = states.astype(jnp.float32)
    means = lax.optimization_barrier(jnp.mean(floats, axis=-1, keepdims=True))
    centered = floats - means
    variance = lax.optimization_barrier(jnp.mean(centered * centered, axis=-1, keepdims=True))
    normed = centered * lax.rsqrt(variance + EPS)
    return (normed * (1.0 + scales[:, None, :]) + shifts[:, None, :]).astype(jnp.bfloat16)

def attend(queries, keys_rows, values_rows):
    step_count, length, columns = queries.shape
    head_count = columns // HEAD_DIM
    block_rows = min(512, length)
    query_heads = queries.astype(jnp.float32).reshape(step_count, length // block_rows, block_rows, head_count, HEAD_DIM).transpose(1, 0, 2, 3, 4)
    key_heads = keys_rows.astype(jnp.float32).reshape(step_count, length, head_count, HEAD_DIM)
    value_heads = values_rows.astype(jnp.float32).reshape(step_count, length, head_count, HEAD_DIM)

    def one_block(query_block):
        scores = jnp.einsum('sbhe,slhe->shbl', query_block, key_heads) * HEAD_DIM ** (-0.5)
        row_max = lax.optimization_barrier(jnp.max(scores, axis=-1, keepdims=True))
        weights = jnp.exp(scores - row_max)
        weights = (weights / lax.optimization_barrier(jnp.sum(weights, axis=-1, keepdims=True))).astype(jnp.bfloat16)
        return jnp.einsum('shbl,slhe->sbhe', weights.astype(jnp.float32), value_heads).astype(jnp.bfloat16)
    blocks = lax.map(one_block, query_heads)
    return blocks.transpose(1, 0, 2, 3, 4).reshape(step_count, length, columns)

def reference(trajectory, initial, step_sizes, time_index, plan, adaln_weight, query_weight, key_weight, value_weight, out_weight):
    shifts, scales = modulation(time_index, plan, adaln_weight)

    def one_step(running, inputs):
        states, shift_row, scale_row, step_size = inputs
        normed = normalize(states[None], shift_row[None], scale_row[None])[0]
        queries = jnp.dot(normed, query_weight, preferred_element_type=jnp.float32).astype(jnp.bfloat16)
        keys_rows = jnp.dot(normed, key_weight, preferred_element_type=jnp.float32).astype(jnp.bfloat16)
        values_rows = jnp.dot(normed, value_weight, preferred_element_type=jnp.float32).astype(jnp.bfloat16)
        attended = attend(queries[None], keys_rows[None], values_rows[None])[0]
        drift = jnp.dot(attended, out_weight, preferred_element_type=jnp.float32)
        running = running + step_size * drift
        return (running, running)
    final_state, updated = lax.scan(one_step, initial.astype(jnp.float32), (trajectory, shifts, scales, step_sizes))
    return updated
```

```python
import functools

import jax
import jax.numpy as jnp
from jax import lax
from jax.experimental import pallas as pl
from jax.experimental.pallas import tpu as pltpu
from jax.sharding import PartitionSpec as P

HEAD_DIM = 64
EPS = 1e-06
BF16 = jnp.bfloat16
F32 = jnp.float32
MIB = 1024 * 1024
VMEM = pl.BlockSpec(memory_space=pltpu.VMEM)
SMEM = pl.BlockSpec(memory_space=pltpu.SMEM)


def modulation(time_index, plan, adaln_weight):
    table_size = plan.shape[0]
    onehot = (time_index[:, None] == jnp.arange(table_size, dtype=jnp.int32)[None, :]).astype(F32)
    sigmas = jnp.sum(onehot * plan[None, :], axis=1)
    half_width = adaln_weight.shape[0] // 2
    frequency = 0.25 * jnp.exp(4.0 * jnp.arange(half_width, dtype=F32) / half_width)
    angles = jnp.log(sigmas)[:, None] * frequency[None, :]
    embedding = jnp.concatenate([jnp.cos(angles), jnp.sin(angles)], axis=1).astype(BF16)
    modulated = jnp.dot(embedding, adaln_weight, preferred_element_type=F32)
    feature_width = adaln_weight.shape[1] // 2
    return (modulated[:, :feature_width], modulated[:, feature_width:])


def project_kernel(mine_ref, other_ref, shift_ref, gain_ref, weight_ref, out_ref, normed_ref):
    rows = mine_ref.shape[0]
    for part, ref in enumerate((mine_ref, other_ref)):
        floats = ref[...].astype(F32)
        centered = floats - jnp.mean(floats, axis=-1, keepdims=True)
        variance = jnp.mean(centered * centered, axis=-1, keepdims=True)
        normed = centered * lax.rsqrt(variance + EPS)
        normed_ref[part * rows : (part + 1) * rows, :] = (
            normed * gain_ref[...] + shift_ref[...]
        ).astype(BF16)
    out_ref[...] = jnp.dot(
        normed_ref[...], weight_ref[...], preferred_element_type=F32
    ).astype(BF16)


def project(mine, other, shift, gain, weight):
    rows, width = mine.shape
    columns = weight.shape[1]
    return pl.pallas_call(
        project_kernel,
        out_shape=jax.ShapeDtypeStruct((2 * rows, columns), BF16),
        in_specs=[VMEM] * 5,
        out_specs=VMEM,
        scratch_shapes=[pltpu.VMEM((2 * rows, width), BF16)],
        compiler_params=pltpu.CompilerParams(vmem_limit_bytes=24 * MIB),
        cost_estimate=pl.CostEstimate(
            flops=4 * rows * width * columns,
            bytes_accessed=4 * rows * width + 2 * width * columns,
            transcendentals=0,
        ),
        name="project",
    )(mine, other, shift, gain, weight)


def attend_kernel(place_ref, *refs):
    parts = refs[:4]
    out_ref, keys_ref, values_ref = refs[4:]
    rows = parts[0].shape[0]
    pair = 2 * HEAD_DIM
    for position, part in enumerate(parts):
        span = slice(position * rows, (position + 1) * rows)
        keys_ref[span, :] = part[:, pair : 2 * pair]
        values_ref[span, :pair] = part[:, 2 * pair :]
    values_ref[:, pair:] = jnp.ones((4 * rows, pair), BF16)
    first = lax.broadcasted_iota(jnp.int32, (1, pair), 1) < HEAD_DIM
    scale = HEAD_DIM ** (-0.5)
    half = rows // 2
    for position, part in enumerate(parts):
        queries = part[:, :pair].astype(F32) * scale
        heads = []
        for mask in (first, jnp.logical_not(first)):
            chosen = jnp.where(mask, queries, 0.0).astype(BF16)
            scores = lax.dot_general(
                chosen, keys_ref[...], (((1,), (1,)), ((), ())), preferred_element_type=F32
            )
            weights = jnp.exp(scores - jnp.max(scores, axis=-1, keepdims=True)).astype(BF16)
            summed = jnp.dot(weights, values_ref[...], preferred_element_type=F32)
            heads.append(summed[:, :pair] / summed[:, pair:])
        attended = jnp.where(first, heads[0], heads[1]).astype(BF16)
        out_ref[place_ref[2 * position]] = attended[:half]
        out_ref[place_ref[2 * position + 1]] = attended[half:]


def attend(place, parts):
    rows = parts[0].shape[0]
    pair = 2 * HEAD_DIM
    return pl.pallas_call(
        attend_kernel,
        out_shape=jax.ShapeDtypeStruct((8, rows // 2, pair), BF16),
        in_specs=[SMEM] + [VMEM] * 4,
        out_specs=VMEM,
        scratch_shapes=[pltpu.VMEM((4 * rows, pair), BF16), pltpu.VMEM((4 * rows, 2 * pair), BF16)],
        compiler_params=pltpu.CompilerParams(vmem_limit_bytes=32 * MIB),
        cost_estimate=pl.CostEstimate(
            flops=16 * 16 * rows * rows * pair,
            bytes_accessed=8 * rows * 3 * pair,
            transcendentals=2 * 16 * rows * rows,
        ),
        name="attend",
    )(place, *parts)


def earlier_kernel(sums_ref, out_ref):
    running = jnp.zeros(sums_ref.shape[1:], F32)
    for index in range(sums_ref.shape[0]):
        out_ref[index] = running.astype(BF16)
        running = running + sums_ref[index].astype(F32)


def earlier(sums):
    return pl.pallas_call(
        earlier_kernel,
        out_shape=jax.ShapeDtypeStruct(sums.shape, BF16),
        in_specs=[VMEM],
        out_specs=VMEM,
        name="earlier",
    )(sums)


def side_by_side(blocks_ref):
    return jnp.concatenate([blocks_ref[index] for index in range(blocks_ref.shape[0])], axis=1)


def own_kernel(sizes_ref, first_ref, second_ref, weight_ref, initial_ref, out_ref):
    rows = initial_ref.shape[0]
    both = jnp.concatenate([side_by_side(first_ref), side_by_side(second_ref)], axis=0)
    drift = jnp.dot(both, weight_ref[...], preferred_element_type=F32)
    start = initial_ref[...].astype(F32) + sizes_ref[0] * drift[:rows]
    out_ref[0] = start
    out_ref[1] = start + sizes_ref[1] * drift[rows:]


def own_terms(sizes, first, second, weight, initial):
    rows, width = initial.shape
    tile = 512
    blocks = pl.BlockSpec(first.shape, lambda n: (0, 0, 0))
    return pl.pallas_call(
        own_kernel,
        out_shape=jax.ShapeDtypeStruct((2, rows, width), F32),
        grid=(width // tile,),
        in_specs=[
            SMEM,
            blocks,
            blocks,
            pl.BlockSpec((weight.shape[0], tile), lambda n: (0, n)),
            pl.BlockSpec((rows, tile), lambda n: (0, n)),
        ],
        out_specs=pl.BlockSpec((2, rows, tile), lambda n: (0, 0, n)),
        compiler_params=pltpu.CompilerParams(vmem_limit_bytes=24 * MIB),
        cost_estimate=pl.CostEstimate(
            flops=4 * rows * weight.shape[0] * width,
            bytes_accessed=2 * weight.size + 8 * rows * width,
            transcendentals=0,
        ),
        name="own_terms",
    )(sizes, first, second, weight, initial)


def total_kernel(before_ref, weight_ref, own_ref, out_ref):
    drift = jnp.dot(side_by_side(before_ref), weight_ref[...], preferred_element_type=F32)
    out_ref[0] = own_ref[0] + drift
    out_ref[1] = own_ref[1] + drift


def totals(before, weight, own):
    _, rows, width = own.shape
    tile = 512
    return pl.pallas_call(
        total_kernel,
        out_shape=jax.ShapeDtypeStruct(own.shape, F32),
        grid=(width // tile,),
        in_specs=[
            pl.BlockSpec(before.shape, lambda n: (0, 0, 0)),
            pl.BlockSpec((weight.shape[0], tile), lambda n: (0, n)),
            pl.BlockSpec((2, rows, tile), lambda n: (0, 0, n)),
        ],
        out_specs=pl.BlockSpec((2, rows, tile), lambda n: (0, 0, n)),
        compiler_params=pltpu.CompilerParams(vmem_limit_bytes=24 * MIB),
        name="totals",
    )(before, weight, own)


def local(
    trajectory,
    initial,
    step_sizes,
    time_index,
    plan,
    adaln_weight,
    query_weight,
    key_weight,
    value_weight,
    out_weight,
):
    groups = lax.axis_size("step")
    fields = lax.axis_size("seq")
    chips = fields // 2
    place = lax.axis_index("seq")
    pair = 2 * HEAD_DIM
    swap = [(i, i ^ 1) for i in range(fields)]

    out_full = lax.all_gather(out_weight, "step", axis=0, tiled=True)

    shifts_by = (1, chips - 1, 2)
    fetched = []
    for step in range(2):
        fetched.append(
            [trajectory[step]]
            + [
                lax.ppermute(
                    trajectory[step], "seq", [(i, (i + 2 * by) % fields) for i in range(fields)]
                )
                for by in shifts_by
            ]
        )
    mine = jnp.concatenate(
        [
            lax.dynamic_slice_in_dim(weight, place * pair, pair, axis=1)
            for weight in (query_weight, key_weight, value_weight)
        ],
        axis=1,
    )
    weight = lax.all_to_all(
        jnp.broadcast_to(mine[None], (groups,) + mine.shape), "step", 0, 0
    ).reshape(-1, mine.shape[1])

    shifts, scales = modulation(time_index, plan, adaln_weight)
    gains = 1.0 + scales

    chip, core = place // 2, place % 2
    source_chips = [chip] + [(chip - by) % chips for by in shifts_by]
    places = jnp.stack(
        [spot for source in source_chips for spot in (2 * source + core, 2 * source + 1 - core)]
    ).astype(jnp.int32)

    gathered = []
    for step in range(2):
        parts = []
        for block in fetched[step]:
            other = lax.ppermute(block, "seq", swap)
            parts.append(
                project(block, other, shifts[step][None], gains[step][None], weight)
            )
        attended = attend(places, parts)
        gathered.append(lax.all_to_all(attended, "seq", 0, 0))

    first, second = gathered
    sums = step_sizes[0] * first.astype(F32) + step_sizes[1] * second.astype(F32)
    slices = sums.astype(BF16).reshape(groups, -1, pair)
    before = lax.all_to_all(earlier(lax.all_to_all(slices, "step", 0, 0)), "step", 0, 0)
    own = own_terms(step_sizes, first, second, out_full, initial)
    return totals(before.reshape(first.shape), out_full, own)


def solution(mesh):
    in_specs = (
        P("step", "seq", None),
        P("seq", None),
        P("step"),
        P("step"),
        P(),
        P(),
        P("step", None),
        P("step", None),
        P("step", None),
        P("step", None),
    )
    out_specs = P("step", "seq", None)
    return jax.shard_map(local, mesh=mesh, in_specs=in_specs, out_specs=out_specs, check_vma=False)
```

```python
import functools

import jax
import jax.numpy as jnp
from jax import lax
from jax.experimental import pallas as pl
from jax.experimental.pallas import tpu as pltpu
from jax.sharding import PartitionSpec as P

HEAD_DIM = 64
EPS = 1e-06
BF16 = jnp.bfloat16
F32 = jnp.float32
MIB = 1024 * 1024
VMEM = pl.BlockSpec(memory_space=pltpu.VMEM)
SMEM = pl.BlockSpec(memory_space=pltpu.SMEM)
HBM = pl.BlockSpec(memory_space=pl.ANY)


def modulation(time_index, plan, adaln_weight):
    table_size = plan.shape[0]
    onehot = (time_index[:, None] == jnp.arange(table_size, dtype=jnp.int32)[None, :]).astype(F32)
    sigmas = jnp.sum(onehot * plan[None, :], axis=1)
    half_width = adaln_weight.shape[0] // 2
    frequency = 0.25 * jnp.exp(4.0 * jnp.arange(half_width, dtype=F32) / half_width)
    angles = jnp.log(sigmas)[:, None] * frequency[None, :]
    embedding = jnp.concatenate([jnp.cos(angles), jnp.sin(angles)], axis=1).astype(BF16)
    modulated = jnp.dot(embedding, adaln_weight, preferred_element_type=F32)
    feature_width = adaln_weight.shape[1] // 2
    return (modulated[:, :feature_width], modulated[:, feature_width:])


def pick_kernel(place_ref, query_ref, key_ref, value_ref, out_weight_ref, picked_ref):
    pair = picked_ref.shape[-1]
    column = pl.multiple_of(place_ref[0] * pair, pair)
    blocks = [ref[:, pl.ds(column, pair)] for ref in (query_ref, key_ref, value_ref)]
    for half in range(2):
        start = pl.multiple_of((2 * place_ref[0] + half) * pair, pair)
        blocks.append(out_weight_ref[:, pl.ds(start, pair)])
    picked = jnp.concatenate(blocks, axis=0)
    for copy in range(picked_ref.shape[0]):
        picked_ref[copy] = picked


def pick(place, query_weight, key_weight, value_weight, out_weight, copies):
    pair = 2 * HEAD_DIM
    rows = 3 * query_weight.shape[0] + 2 * out_weight.shape[0]
    return pl.pallas_call(
        pick_kernel,
        out_shape=jax.ShapeDtypeStruct((copies, rows, pair), BF16),
        in_specs=[SMEM] + [VMEM] * 4,
        out_specs=VMEM,
        compiler_params=pltpu.CompilerParams(vmem_limit_bytes=60 * MIB),
        name="pick",
    )(place, query_weight, key_weight, value_weight, out_weight)


def place_kernel(place_ref, *refs):
    blocks, (weight_ref, out_weight_ref) = refs[:-2], refs[-2:]
    height, low = weight_ref.shape[2], out_weight_ref.shape[2]
    pair = blocks[0].shape[2]
    for k, ref in enumerate(blocks):
        for part in range(3):
            weight_ref[:, place_ref[k], :, part * pair : (part + 1) * pair] = ref[
                :, part * height : (part + 1) * height
            ]
        for part in range(2):
            start = 3 * height + part * low
            out_weight_ref[:, place_ref[k], :, part * pair : (part + 1) * pair] = ref[
                :, start : start + low
            ]


def place_columns(place, blocks, height, low):
    depth, _, pair = blocks[0].shape
    across = len(blocks)
    weight, out_weight = pl.pallas_call(
        place_kernel,
        out_shape=(
            jax.ShapeDtypeStruct((depth, across, height, 3 * pair), BF16),
            jax.ShapeDtypeStruct((depth, across, low, 2 * pair), BF16),
        ),
        in_specs=[SMEM] + [VMEM] * across,
        out_specs=(VMEM, VMEM),
        compiler_params=pltpu.CompilerParams(vmem_limit_bytes=16 * MIB),
        name="place",
    )(place, *blocks)
    return weight.reshape(-1, 3 * pair), out_weight.reshape(-1, 2 * pair)


def normalize(rows, gain, shift):
    floats = rows.astype(F32)
    centered = floats - jnp.mean(floats, axis=-1, keepdims=True)
    variance = jnp.mean(centered * centered, axis=-1, keepdims=True)
    normed = centered * lax.rsqrt(variance + EPS)
    return (normed * gain + shift).astype(BF16)


def project_rows(loads, raw_ref, normed_ref, gain_ref, shift_ref, ready, weight_ref, store):
    rows = raw_ref.shape[1]
    groups = raw_ref.shape[0] // 4
    for group in range(groups):
        for step in range(2):
            slot = (2 * group + step) % 2
            for side in range(2):
                index = 4 * group + 2 * step + side
                loads[index].wait()
                normed_ref[slot, side * rows : (side + 1) * rows, :] = normalize(
                    raw_ref[index], gain_ref[step : step + 1], shift_ref[step : step + 1]
                )
            if group == 0 and step == 0:
                ready()
            store(
                group,
                step,
                jnp.dot(
                    normed_ref[slot], weight_ref[...], preferred_element_type=F32
                ).astype(BF16),
            )


def start_loads(sources, raw_ref, sems):
    loads = [
        pltpu.make_async_copy(source, raw_ref.at[index], sems.at[index])
        for index, source in enumerate(sources)
    ]
    for load in loads:
        load.start()
    return loads


def project_kernel(shift_ref, gain_ref, weight_source, *refs):
    blocks, (out_ref, raw_ref, normed_ref, weight_ref, sems, weight_sem) = refs[:-6], refs[-6:]
    fetch = pltpu.make_async_copy(weight_source, weight_ref, weight_sem)
    sources = [
        blocks[2 * group + side].at[step]
        for group in range(len(blocks) // 2)
        for step in range(2)
        for side in range(2)
    ]
    loads = start_loads(sources, raw_ref, sems)
    fetch.start()

    def store(group, step, value):
        out_ref[group, step] = value

    project_rows(
        loads, raw_ref, normed_ref, gain_ref, shift_ref, fetch.wait, weight_ref, store
    )


def project(shift, gain, weight, blocks):
    _, rows, width = blocks[0].shape
    columns = weight.shape[1]
    groups = len(blocks) // 2
    return pl.pallas_call(
        project_kernel,
        out_shape=jax.ShapeDtypeStruct((groups, 2, 2 * rows, columns), BF16),
        in_specs=[VMEM] * 2 + [HBM] * (1 + len(blocks)),
        out_specs=VMEM,
        scratch_shapes=[
            pltpu.VMEM((4 * groups, rows, width), BF16),
            pltpu.VMEM((2, 2 * rows, width), BF16),
            pltpu.VMEM(weight.shape, BF16),
            pltpu.SemaphoreType.DMA((4 * groups,)),
            pltpu.SemaphoreType.DMA,
        ],
        compiler_params=pltpu.CompilerParams(vmem_limit_bytes=40 * MIB),
        cost_estimate=pl.CostEstimate(
            flops=8 * groups * rows * width * columns,
            bytes_accessed=8 * groups * rows * width + 2 * width * columns,
            transcendentals=0,
        ),
        name="project",
    )(shift, gain, weight, *blocks)


def attend_kernel(place_ref, sizes_ref, shift_ref, gain_ref, parts_ref, weight_source, *refs):
    blocks, outs = refs[:4], refs[4:8]
    (
        sums_ref,
        last_ref,
        keys_ref,
        values_ref,
        block_ref,
        order_ref,
        raw_ref,
        normed_ref,
        weight_ref,
        sems,
        weight_sem,
    ) = refs[8:]
    fetch = pltpu.make_async_copy(weight_source, weight_ref, weight_sem)
    sources = [blocks[2 * side + step].at[0] for step in range(2) for side in range(2)]
    loads = start_loads(sources, raw_ref, sems)
    fetch.start()

    def store(group, step, value):
        last_ref[step] = value

    project_rows(
        loads, raw_ref, normed_ref, gain_ref, shift_ref, fetch.wait, weight_ref, store
    )

    known, steps, rows, _ = parts_ref.shape
    pair = 2 * HEAD_DIM
    half = rows // 2
    first = lax.broadcasted_iota(jnp.int32, (1, pair), 1) < HEAD_DIM
    scale = HEAD_DIM ** (-0.5)
    values_ref[:, pair:] = jnp.ones((4 * rows, pair), BF16)
    for step in range(steps):
        parts = [parts_ref.at[position, step] for position in range(known)] + [last_ref.at[step]]
        for position, part in enumerate(parts):
            span = slice(position * rows, (position + 1) * rows)
            keys_ref[span, :] = part[:, pair : 2 * pair]
            values_ref[span, :pair] = part[:, 2 * pair :]
        for position, part in enumerate(parts):
            queries = part[:, :pair].astype(F32) * scale
            heads = []
            for mask in (first, jnp.logical_not(first)):
                chosen = jnp.where(mask, queries, 0.0).astype(BF16)
                scores = lax.dot_general(
                    chosen, keys_ref[...], (((1,), (1,)), ((), ())), preferred_element_type=F32
                )
                weights = jnp.exp(scores - jnp.max(scores, axis=-1, keepdims=True)).astype(BF16)
                summed = jnp.dot(weights, values_ref[...], preferred_element_type=F32)
                heads.append(summed[:, :pair] / summed[:, pair:])
            attended = jnp.where(first, heads[0], heads[1]).astype(BF16)
            for side in range(2):
                block = attended[side * half : (side + 1) * half]
                spot = place_ref[2 * position + side]
                outs[position][side, step] = block
                scaled = sizes_ref[step] * block.astype(F32)
                if step == 0:
                    block_ref[spot] = scaled
                else:
                    block_ref[spot] = block_ref[spot] + scaled
    groups = sums_ref.shape[0]
    depth = sums_ref.shape[1]
    per = half // groups
    for field in range(block_ref.shape[0]):
        for turn in range(per):
            order_ref[pl.ds(per * field + turn, groups, stride=depth), :] = block_ref[
                field, turn * groups : (turn + 1) * groups
            ]
    sums_ref[...] = order_ref[...].astype(BF16).reshape(sums_ref.shape)


def attend(place, sizes, shift, gain, parts, weight, blocks, groups):
    _, steps, rows, columns = parts.shape
    pair = 2 * HEAD_DIM
    length = 4 * rows
    width = weight.shape[0]
    block = jax.ShapeDtypeStruct((2, steps, rows // 2, pair), BF16)
    *outs, sums = pl.pallas_call(
        attend_kernel,
        out_shape=(block,) * 4
        + (jax.ShapeDtypeStruct((groups, length // groups, pair), BF16),),
        in_specs=[SMEM] * 2 + [VMEM] * 3 + [HBM] * 5,
        out_specs=(VMEM,) * 5,
        scratch_shapes=[
            pltpu.VMEM((steps, rows, columns), BF16),
            pltpu.VMEM((length, pair), BF16),
            pltpu.VMEM((length, 2 * pair), BF16),
            pltpu.VMEM((8, rows // 2, pair), F32),
            pltpu.VMEM((length, pair), F32),
            pltpu.VMEM((4, rows // 2, width), BF16),
            pltpu.VMEM((2, rows, width), BF16),
            pltpu.VMEM(weight.shape, BF16),
            pltpu.SemaphoreType.DMA((4,)),
            pltpu.SemaphoreType.DMA,
        ],
        compiler_params=pltpu.CompilerParams(vmem_limit_bytes=40 * MIB),
        cost_estimate=pl.CostEstimate(
            flops=16 * 16 * rows * rows * pair + 4 * rows * width * columns,
            bytes_accessed=8 * rows * 3 * pair + 2 * width * columns,
            transcendentals=4 * 16 * rows * rows,
        ),
        name="attend",
    )(place, sizes, shift, gain, parts, weight, *blocks)
    return outs, sums


def earlier_kernel(sums_ref, out_ref):
    running = jnp.zeros(sums_ref.shape[1:], F32)
    for index in range(sums_ref.shape[0]):
        out_ref[index] = running.astype(BF16)
        running = running + sums_ref[index].astype(F32)


def earlier(sums):
    return pl.pallas_call(
        earlier_kernel,
        out_shape=jax.ShapeDtypeStruct(sums.shape, BF16),
        in_specs=[VMEM],
        out_specs=VMEM,
        compiler_params=pltpu.CompilerParams(vmem_limit_bytes=16 * MIB),
        name="earlier",
    )(sums)


def total_kernel(place_ref, heads_ref, sizes_ref, before_ref, initial_ref, *refs):
    blocks, tiles = refs[:8], refs[8:16]
    out_ref, order_ref, rows_ref, weight_ref, result_ref, load_sems, store_sems = refs[16:]
    groups, depth, pair = before_ref.shape
    rows = initial_ref.shape[0]
    per = rows // groups
    width = weight_ref.shape[-1]
    loads = [
        pltpu.make_async_copy(source, weight_ref.at[index], load_sems.at[index])
        for index, source in enumerate(tiles)
    ]
    for load in loads:
        load.start()

    order_ref[...] = before_ref[...].astype(F32).reshape(order_ref.shape)
    for field in range(depth // per):
        columns = slice(field * pair, (field + 1) * pair)
        for turn in range(per):
            rows_ref[turn * groups : (turn + 1) * groups, columns] = order_ref[
                pl.ds(per * field + turn, groups, stride=depth), :
            ].astype(BF16)
    for index, ref in enumerate(blocks):
        start = pl.multiple_of(heads_ref[index] * pair, pair)
        for step in range(2):
            rows_ref[(1 + step) * rows : (2 + step) * rows, pl.ds(start, pair)] = ref[
                index // 4, step
            ]

    stores = []
    for index, load in enumerate(loads):
        load.wait()
        start = pl.multiple_of(place_ref[index] * width, width)
        drift = jnp.dot(rows_ref[...], weight_ref[index], preferred_element_type=F32)
        base = (
            initial_ref[:, pl.ds(start, width)].astype(F32)
            + drift[:rows]
            + sizes_ref[0] * drift[rows : 2 * rows]
        )
        result_ref[index, 0] = base
        result_ref[index, 1] = base + sizes_ref[1] * drift[2 * rows :]
        store = pltpu.make_async_copy(
            result_ref.at[index], out_ref.at[:, :, pl.ds(start, width)], store_sems.at[index]
        )
        store.start()
        stores.append(store)
    for store in stores:
        store.wait()


def totals(place, heads, sizes, before, initial, blocks, tiles):
    rows, width = initial.shape
    groups, depth, pair = before.shape
    count = len(tiles)
    return pl.pallas_call(
        total_kernel,
        out_shape=jax.ShapeDtypeStruct((2, rows, width), F32),
        in_specs=[SMEM] * 3 + [VMEM] * 10 + [HBM] * 8,
        out_specs=HBM,
        scratch_shapes=[
            pltpu.VMEM((groups * depth, pair), F32),
            pltpu.VMEM((3 * rows, tiles[0].shape[0]), BF16),
            pltpu.VMEM((count,) + tiles[0].shape, BF16),
            pltpu.VMEM((count, 2, rows, tiles[0].shape[1]), F32),
            pltpu.SemaphoreType.DMA((count,)),
            pltpu.SemaphoreType.DMA((count,)),
        ],
        compiler_params=pltpu.CompilerParams(vmem_limit_bytes=60 * MIB),
        name="totals",
    )(place, heads, sizes, before, initial, *blocks, *tiles)


def gather_depth(blocks, shape):
    return lax.all_to_all(
        blocks,
        "step",
        0,
        0,
        axis_index_groups=[[x + shape[1] * z for z in range(shape[0])] for x in range(shape[1])],
    )


def fetch_column(block, shape, by):
    across = shape[1]
    return lax.ppermute(
        block,
        "step",
        [(i, i // across * across + (i - by) % across) for i in range(shape[0] * across)],
    )


def local(
    trajectory,
    initial,
    step_sizes,
    time_index,
    plan,
    adaln_weight,
    query_weight,
    key_weight,
    value_weight,
    out_weight,
):
    fields = lax.axis_size("seq")
    groups = lax.axis_size("step")
    chips = fields // 2
    shape = (groups // 4, 4)
    place = lax.axis_index("seq")
    chip, core = place // 2, place % 2
    column = lax.axis_index("step") % 4
    pair = 2 * HEAD_DIM
    swap = [(i, i ^ 1) for i in range(fields)]

    def along_ring(block, by):
        return lax.ppermute(block, "seq", [(i, (i + 2 * by) % fields) for i in range(fields)])

    shifts_by = (1, chips - 1, 2)
    picked = pick(
        place[None].astype(jnp.int32),
        query_weight,
        key_weight,
        value_weight,
        out_weight,
        shape[0],
    )
    along = gather_depth(picked, shape)
    weights = [along] + [fetch_column(along, shape, by) for by in range(1, shape[1])]

    behind = along_ring(trajectory, 1)
    ahead = along_ring(trajectory, chips - 1)
    opposite = (along_ring(behind[:1], 1), along_ring(ahead[1:], chips - 1))

    shifts, scales = modulation(time_index, plan, adaln_weight)
    gains = 1.0 + scales

    columns = jnp.stack([(column + by) % 4 for by in range(4)]).astype(jnp.int32)
    source_chips = [chip] + [(chip - by) % chips for by in shifts_by]
    places = jnp.stack(
        [spot for source in source_chips for spot in (2 * source + core, 2 * source + 1 - core)]
    ).astype(jnp.int32)

    weight, out_tile = place_columns(
        columns, weights, query_weight.shape[0], out_weight.shape[0]
    )

    def partner_of(block, after):
        block, _ = lax.optimization_barrier((block, after))
        return lax.ppermute(block, "seq", swap)

    blocks = []
    for block in (trajectory, behind, ahead):
        blocks += [block, partner_of(block, weights)]
    parts = project(shifts, gains, weight, blocks)
    others = tuple(partner_of(block, parts) for block in opposite)
    out_tile, _ = lax.optimization_barrier((out_tile, parts))
    out_tiles = [out_tile] + [along_ring(out_tile, by) for by in shifts_by]
    attended, sums = attend(
        places, step_sizes, shifts, gains, parts, weight, opposite + others, groups
    )
    out_tiles, _ = lax.optimization_barrier((out_tiles, sums))
    out_tiles = out_tiles + [lax.ppermute(tile, "seq", swap) for tile in out_tiles]
    per = sums.shape[1] // fields
    received = lax.all_to_all(
        sums.reshape(groups * fields, per, pair), ("step", "seq"), 0, 0
    ).reshape(sums.shape)
    before = lax.all_to_all(earlier(received), "step", 0, 0)

    arrived = [attended[0]] + [
        along_ring(block, chips - by) for block, by in zip(attended[1:], shifts_by)
    ]
    arrived = arrived + [lax.ppermute(block, "seq", swap) for block in arrived]
    sources = [chip] + [(chip + by) % chips for by in shifts_by]
    heads = jnp.stack(
        [2 * source + core for source in sources] + [2 * source + 1 - core for source in sources]
    ).astype(jnp.int32)
    spots = jnp.concatenate([places[0::2], places[1::2]])
    return totals(spots, heads, step_sizes, before, initial, arrived, out_tiles)


def solution(mesh):
    in_specs = (
        P("step", "seq", None),
        P("seq", None),
        P("step"),
        P("step"),
        P(),
        P(),
        P("step", None),
        P("step", None),
        P("step", None),
        P("step", None),
    )
    out_specs = P("step", "seq", None)
    return jax.shard_map(local, mesh=mesh, in_specs=in_specs, out_specs=out_specs, check_vma=False)
```

```python
import functools

import jax
import jax.numpy as jnp
from jax import lax
from jax.experimental import pallas as pl
from jax.experimental.pallas import tpu as pltpu
from jax.sharding import PartitionSpec as P

HEAD_DIM = 64
EPS = 1e-06
BF16 = jnp.bfloat16
F32 = jnp.float32
MIB = 1024 * 1024
VMEM = pl.BlockSpec(memory_space=pltpu.VMEM)
SMEM = pl.BlockSpec(memory_space=pltpu.SMEM)
HBM = pl.BlockSpec(memory_space=pl.ANY)


def modulation(time_index, plan, adaln_weight):
    table_size = plan.shape[0]
    onehot = (time_index[:, None] == jnp.arange(table_size, dtype=jnp.int32)[None, :]).astype(F32)
    sigmas = jnp.sum(onehot * plan[None, :], axis=1)
    half_width = adaln_weight.shape[0] // 2
    frequency = 0.25 * jnp.exp(4.0 * jnp.arange(half_width, dtype=F32) / half_width)
    angles = jnp.log(sigmas)[:, None] * frequency[None, :]
    embedding = jnp.concatenate([jnp.cos(angles), jnp.sin(angles)], axis=1).astype(BF16)
    modulated = jnp.dot(embedding, adaln_weight, preferred_element_type=F32)
    feature_width = adaln_weight.shape[1] // 2
    return (modulated[:, :feature_width], modulated[:, feature_width:])


def pick_kernel(place_ref, query_ref, key_ref, value_ref, out_weight_ref, picked_ref):
    pair = picked_ref.shape[-1] // 4
    column = pl.multiple_of(place_ref[0] * pair, pair)
    blocks = [ref[:, pl.ds(column, pair)] for ref in (query_ref, key_ref, value_ref)]
    halves = []
    for half in range(2):
        start = pl.multiple_of((2 * place_ref[0] + half) * pair, pair)
        halves.append(out_weight_ref[:, pl.ds(start, pair)])
    picked = jnp.concatenate(blocks + [jnp.concatenate(halves, axis=0)], axis=1)
    for copy in range(picked_ref.shape[0]):
        picked_ref[copy] = picked


def pick(place, query_weight, key_weight, value_weight, out_weight, copies):
    rows = query_weight.shape[0]
    return pl.pallas_call(
        pick_kernel,
        out_shape=jax.ShapeDtypeStruct((copies, rows, 8 * HEAD_DIM), BF16),
        in_specs=[SMEM] + [VMEM] * 4,
        out_specs=VMEM,
        compiler_params=pltpu.CompilerParams(vmem_limit_bytes=60 * MIB),
        name="pick",
    )(place, query_weight, key_weight, value_weight, out_weight)


def normalize_kernel(shift_ref, gain_ref, rows_ref, out_ref):
    for step in range(2):
        floats = rows_ref[step].astype(F32)
        centered = floats - jnp.mean(floats, axis=-1, keepdims=True)
        variance = jnp.mean(centered * centered, axis=-1, keepdims=True)
        normed = centered * lax.rsqrt(variance + EPS)
        out_ref[step] = (normed * gain_ref[step : step + 1] + shift_ref[step : step + 1]).astype(
            BF16
        )


def normalize(shift, gain, rows):
    return pl.pallas_call(
        normalize_kernel,
        out_shape=jax.ShapeDtypeStruct(rows.shape, BF16),
        in_specs=[VMEM] * 3,
        out_specs=VMEM,
        compiler_params=pltpu.CompilerParams(vmem_limit_bytes=24 * MIB),
        cost_estimate=pl.CostEstimate(
            flops=16 * rows.size, bytes_accessed=8 * rows.size, transcendentals=0
        ),
        name="normalize",
    )(shift, gain, rows)


def tile_kernel(source_ref, tile_ref, half_ref, sems):
    pair = half_ref.shape[-1]
    across = half_ref.shape[0]
    start = source_ref.shape[-1] - pair
    loads = [
        pltpu.make_async_copy(
            source_ref.at[x, :, :, pl.ds(start, pair)], half_ref.at[x], sems.at[x]
        )
        for x in range(across)
    ]
    for load in loads:
        load.start()
    low = tile_ref.shape[2]
    for x, load in enumerate(loads):
        load.wait()
        for half in range(2):
            tile_ref[:, x, :, half * pair : (half + 1) * pair] = half_ref[
                x, :, half * low : (half + 1) * low
            ]


def tile_of(weights):
    across, depth, height, columns = weights.shape
    pair = columns // 4
    return pl.pallas_call(
        tile_kernel,
        out_shape=jax.ShapeDtypeStruct((depth, across, height // 2, 2 * pair), BF16),
        in_specs=[HBM],
        out_specs=VMEM,
        scratch_shapes=[
            pltpu.VMEM((across, depth, height, pair), BF16),
            pltpu.SemaphoreType.DMA((across,)),
        ],
        compiler_params=pltpu.CompilerParams(vmem_limit_bytes=60 * MIB),
        name="tile",
    )(weights).reshape(-1, 2 * pair)


def attend_kernel(place_ref, sizes_ref, source_ref, *refs):
    blocks, outs = refs[:10], refs[10:14]
    (
        sums_ref,
        parts_ref,
        keys_ref,
        values_ref,
        block_ref,
        order_ref,
        rows_ref,
        weight_ref,
        sems,
        weight_sems,
    ) = refs[14:]
    steps, groups, rows, width = rows_ref.shape
    pair = 2 * HEAD_DIM
    half = rows // 2

    fetches = [
        pltpu.make_async_copy(source_ref.at[x], weight_ref.at[:, x], weight_sems.at[x])
        for x in range(source_ref.shape[0])
    ]
    units = []
    for step in range(steps):
        for group in range(groups):
            pairs = []
            for side in range(2):
                if group < 3:
                    source = blocks[2 * group + side].at[step]
                else:
                    source = blocks[6 + 2 * side + step].at[0]
                pairs.append(
                    pltpu.make_async_copy(
                        source,
                        rows_ref.at[step, group, pl.ds(side * half, half)],
                        sems.at[step, group, side],
                    )
                )
            units.append(pairs)

    def start(unit):
        for load in units[unit] if unit < len(units) else []:
            load.start()

    for fetch in fetches:
        fetch.start()
    for unit in range(2):
        start(unit)
    values_ref[:, pair:] = jnp.ones((groups * rows, pair), BF16)
    for fetch in fetches:
        fetch.wait()
    for unit in range(2, 4):
        start(unit)

    weight = weight_ref.reshape(width, weight_ref.shape[-1])
    first = lax.broadcasted_iota(jnp.int32, (1, pair), 1) < HEAD_DIM
    scale = HEAD_DIM ** (-0.5)
    for step in range(steps):
        for group in range(groups):
            unit = step * groups + group
            for load in units[unit]:
                load.wait()
            start(unit + 4)
            part = jnp.dot(
                rows_ref[step, group], weight[:, : 3 * pair], preferred_element_type=F32
            ).astype(BF16)
            span = slice(group * rows, (group + 1) * rows)
            parts_ref[span, :] = part[:, :pair]
            keys_ref[span, :] = part[:, pair : 2 * pair]
            values_ref[span, :pair] = part[:, 2 * pair :]
        for position in range(groups):
            queries = parts_ref[position * rows : (position + 1) * rows, :].astype(F32) * scale
            heads = []
            for mask in (first, jnp.logical_not(first)):
                chosen = jnp.where(mask, queries, 0.0).astype(BF16)
                scores = lax.dot_general(
                    chosen, keys_ref[...], (((1,), (1,)), ((), ())), preferred_element_type=F32
                )
                weights = jnp.exp(scores - jnp.max(scores, axis=-1, keepdims=True)).astype(BF16)
                summed = jnp.dot(weights, values_ref[...], preferred_element_type=F32)
                heads.append(summed[:, :pair] / summed[:, pair:])
            attended = jnp.where(first, heads[0], heads[1]).astype(BF16)
            for side in range(2):
                block = attended[side * half : (side + 1) * half]
                spot = place_ref[2 * position + side]
                outs[position][side, step] = block
                scaled = sizes_ref[step] * block.astype(F32)
                if step == 0:
                    block_ref[spot] = scaled
                else:
                    block_ref[spot] = block_ref[spot] + scaled
    targets, depth = sums_ref.shape[:2]
    per = half // targets
    for field in range(block_ref.shape[0]):
        for turn in range(per):
            order_ref[pl.ds(per * field + turn, targets, stride=depth), :] = block_ref[
                field, turn * targets : (turn + 1) * targets
            ]
    sums_ref[...] = order_ref[...].astype(BF16).reshape(sums_ref.shape)


def attend(place, sizes, weights, blocks, targets):
    steps, half, width = blocks[0].shape
    across, depth, height, columns = weights.shape
    pair = columns // 4
    groups, rows = 4, 2 * half
    length = groups * rows
    block = jax.ShapeDtypeStruct((2, steps, half, pair), BF16)
    *outs, sums = pl.pallas_call(
        attend_kernel,
        out_shape=(block,) * groups
        + (jax.ShapeDtypeStruct((targets, length // targets, pair), BF16),),
        in_specs=[SMEM] * 2 + [HBM] * (1 + len(blocks)),
        out_specs=(VMEM,) * (groups + 1),
        scratch_shapes=[
            pltpu.VMEM((length, pair), BF16),
            pltpu.VMEM((length, pair), BF16),
            pltpu.VMEM((length, 2 * pair), BF16),
            pltpu.VMEM((2 * groups, half, pair), F32),
            pltpu.VMEM((length, pair), F32),
            pltpu.VMEM((steps, groups, rows, width), BF16),
            pltpu.VMEM((depth, across, height, columns), BF16),
            pltpu.SemaphoreType.DMA((steps, groups, 2)),
            pltpu.SemaphoreType.DMA((across,)),
        ],
        compiler_params=pltpu.CompilerParams(vmem_limit_bytes=60 * MIB),
        cost_estimate=pl.CostEstimate(
            flops=16 * length * length * pair + 12 * length * width * pair,
            bytes_accessed=4 * length * width + 8 * width * pair,
            transcendentals=4 * length * length,
        ),
        name="attend",
    )(place, sizes, weights, *blocks)
    return outs, sums


def earlier_kernel(sums_ref, out_ref):
    running = jnp.zeros(sums_ref.shape[1:], F32)
    for index in range(sums_ref.shape[0]):
        out_ref[index] = running.astype(BF16)
        running = running + sums_ref[index].astype(F32)


def earlier(sums):
    return pl.pallas_call(
        earlier_kernel,
        out_shape=jax.ShapeDtypeStruct(sums.shape, BF16),
        in_specs=[VMEM],
        out_specs=VMEM,
        compiler_params=pltpu.CompilerParams(vmem_limit_bytes=16 * MIB),
        name="earlier",
    )(sums)


def total_kernel(place_ref, heads_ref, sizes_ref, before_ref, initial_ref, *refs):
    blocks, tiles = refs[:8], refs[8:16]
    out_ref, order_ref, rows_ref, weight_ref, result_ref, load_sems, store_sems = refs[16:]
    groups, depth, pair = before_ref.shape
    rows = initial_ref.shape[0]
    per = rows // groups
    width = weight_ref.shape[-1]
    loads = [
        pltpu.make_async_copy(source, weight_ref.at[index], load_sems.at[index])
        for index, source in enumerate(tiles)
    ]
    for load in loads[:3]:
        load.start()

    order_ref[...] = before_ref[...].astype(F32).reshape(order_ref.shape)
    for field in range(depth // per):
        columns = slice(field * pair, (field + 1) * pair)
        for turn in range(per):
            rows_ref[turn * groups : (turn + 1) * groups, columns] = order_ref[
                pl.ds(per * field + turn, groups, stride=depth), :
            ].astype(BF16)
    for index, ref in enumerate(blocks):
        start = pl.multiple_of(heads_ref[index] * pair, pair)
        for step in range(2):
            rows_ref[(1 + step) * rows : (2 + step) * rows, pl.ds(start, pair)] = ref[
                index // 4, step
            ]

    stores = []
    for index, load in enumerate(loads):
        load.wait()
        for later in loads[index + 3 : index + 4]:
            later.start()
        start = pl.multiple_of(place_ref[index] * width, width)
        drift = jnp.dot(rows_ref[...], weight_ref[index], preferred_element_type=F32)
        base = (
            initial_ref[:, pl.ds(start, width)].astype(F32)
            + drift[:rows]
            + sizes_ref[0] * drift[rows : 2 * rows]
        )
        result_ref[index, 0] = base
        result_ref[index, 1] = base + sizes_ref[1] * drift[2 * rows :]
        store = pltpu.make_async_copy(
            result_ref.at[index], out_ref.at[:, :, pl.ds(start, width)], store_sems.at[index]
        )
        store.start()
        stores.append(store)
    for store in stores:
        store.wait()


def totals(place, heads, sizes, before, initial, blocks, tiles):
    rows, width = initial.shape
    groups, depth, pair = before.shape
    count = len(tiles)
    return pl.pallas_call(
        total_kernel,
        out_shape=jax.ShapeDtypeStruct((2, rows, width), F32),
        in_specs=[SMEM] * 3 + [VMEM] * 10 + [HBM] * 8,
        out_specs=HBM,
        scratch_shapes=[
            pltpu.VMEM((groups * depth, pair), F32),
            pltpu.VMEM((3 * rows, tiles[0].shape[0]), BF16),
            pltpu.VMEM((count,) + tiles[0].shape, BF16),
            pltpu.VMEM((count, 2, rows, tiles[0].shape[1]), F32),
            pltpu.SemaphoreType.DMA((count,)),
            pltpu.SemaphoreType.DMA((count,)),
        ],
        compiler_params=pltpu.CompilerParams(vmem_limit_bytes=60 * MIB),
        name="totals",
    )(place, heads, sizes, before, initial, *blocks, *tiles)


def gather_depth(blocks, shape):
    return lax.all_to_all(
        blocks,
        "step",
        0,
        0,
        axis_index_groups=[[x + shape[1] * z for z in range(shape[0])] for x in range(shape[1])],
    )


def gather_columns(block, shape):
    across = shape[1]
    return lax.all_to_all(
        jnp.broadcast_to(block[None], (across,) + block.shape),
        "step",
        0,
        0,
        axis_index_groups=[[z * across + x for x in range(across)] for z in range(shape[0])],
    )


def local(
    trajectory,
    initial,
    step_sizes,
    time_index,
    plan,
    adaln_weight,
    query_weight,
    key_weight,
    value_weight,
    out_weight,
):
    fields = lax.axis_size("seq")
    groups = lax.axis_size("step")
    chips = fields // 2
    shape = (groups // 4, 4)
    place = lax.axis_index("seq")
    chip, core = place // 2, place % 2
    pair = 2 * HEAD_DIM
    swap = [(i, i ^ 1) for i in range(fields)]

    def along_ring(block, by):
        return lax.ppermute(block, "seq", [(i, (i + 2 * by) % fields) for i in range(fields)])

    shifts_by = (1, chips - 1, 2)
    picked = pick(
        place[None].astype(jnp.int32),
        query_weight,
        key_weight,
        value_weight,
        out_weight,
        shape[0],
    )
    weights = gather_columns(gather_depth(picked, shape), shape)

    shifts, scales = modulation(time_index, plan, adaln_weight)
    gains = 1.0 + scales

    source_chips = [chip] + [(chip - by) % chips for by in shifts_by]
    places = jnp.stack(
        [spot for source in source_chips for spot in (2 * source + core, 2 * source + 1 - core)]
    ).astype(jnp.int32)

    def partner_of(block):
        return lax.ppermute(block, "seq", swap)

    here = normalize(shifts, gains, trajectory)
    behind, ahead = along_ring(here, 1), along_ring(here, chips - 1)
    opposite = [along_ring(behind[:1], 1), along_ring(ahead[1:], chips - 1)]
    blocks = []
    for block in (here, behind, ahead):
        blocks += [block, partner_of(block)]
    blocks += opposite + [partner_of(block) for block in opposite]
    out_tile = tile_of(weights)
    out_tiles = [out_tile] + [along_ring(out_tile, by) for by in shifts_by]
    attended, sums = attend(places, step_sizes, weights, blocks, groups)
    out_tiles, _ = lax.optimization_barrier((out_tiles, sums))
    out_tiles = out_tiles + [partner_of(tile) for tile in out_tiles]

    per = sums.shape[1] // fields
    received = lax.all_to_all(
        sums.reshape(groups * fields, per, pair), ("step", "seq"), 0, 0
    ).reshape(sums.shape)
    before = lax.all_to_all(earlier(received), "step", 0, 0)

    arrived = [attended[0]] + [
        along_ring(block, chips - by) for block, by in zip(attended[1:], shifts_by)
    ]
    arrived = arrived + [partner_of(block) for block in arrived]
    sources = [chip] + [(chip + by) % chips for by in shifts_by]
    heads = jnp.stack(
        [2 * source + core for source in sources] + [2 * source + 1 - core for source in sources]
    ).astype(jnp.int32)
    spots = jnp.concatenate([places[0::2], places[1::2]])
    return totals(spots, heads, step_sizes, before, initial, arrived, out_tiles)


def solution(mesh):
    in_specs = (
        P("step", "seq", None),
        P("seq", None),
        P("step"),
        P("step"),
        P(),
        P(),
        P("step", None),
        P("step", None),
        P("step", None),
        P("step", None),
    )
    out_specs = P("step", "seq", None)
    return jax.shard_map(local, mesh=mesh, in_specs=in_specs, out_specs=out_specs, check_vma=False)
```

```python
import functools

import jax
import jax.numpy as jnp
from jax import lax
from jax.experimental import pallas as pl
from jax.experimental.pallas import tpu as pltpu
from jax.sharding import PartitionSpec as P

HEAD_DIM = 64
EPS = 1e-06
BF16 = jnp.bfloat16
F32 = jnp.float32
MIB = 1024 * 1024
VMEM = pl.BlockSpec(memory_space=pltpu.VMEM)
SMEM = pl.BlockSpec(memory_space=pltpu.SMEM)
HBM = pl.BlockSpec(memory_space=pl.ANY)


def modulation(time_index, plan, adaln_weight):
    table_size = plan.shape[0]
    onehot = (time_index[:, None] == jnp.arange(table_size, dtype=jnp.int32)[None, :]).astype(F32)
    sigmas = jnp.sum(onehot * plan[None, :], axis=1)
    half_width = adaln_weight.shape[0] // 2
    frequency = 0.25 * jnp.exp(4.0 * jnp.arange(half_width, dtype=F32) / half_width)
    angles = jnp.log(sigmas)[:, None] * frequency[None, :]
    embedding = jnp.concatenate([jnp.cos(angles), jnp.sin(angles)], axis=1).astype(BF16)
    modulated = jnp.dot(embedding, adaln_weight, preferred_element_type=F32)
    feature_width = adaln_weight.shape[1] // 2
    return (modulated[:, :feature_width], modulated[:, feature_width:])


def pick_kernel(place_ref, query_ref, key_ref, value_ref, out_weight_ref, picked_ref):
    pair = picked_ref.shape[-1] // 4
    column = pl.multiple_of(place_ref[0] * pair, pair)
    blocks = [ref[:, pl.ds(column, pair)] for ref in (query_ref, key_ref, value_ref)]
    halves = []
    for half in range(2):
        start = pl.multiple_of((2 * place_ref[0] + half) * pair, pair)
        halves.append(out_weight_ref[:, pl.ds(start, pair)])
    picked = jnp.concatenate(blocks + [jnp.concatenate(halves, axis=0)], axis=1)
    for copy in range(picked_ref.shape[0]):
        picked_ref[copy] = picked


def pick(place, query_weight, key_weight, value_weight, out_weight, copies):
    rows = query_weight.shape[0]
    return pl.pallas_call(
        pick_kernel,
        out_shape=jax.ShapeDtypeStruct((copies, rows, 8 * HEAD_DIM), BF16),
        in_specs=[SMEM] + [VMEM] * 4,
        out_specs=VMEM,
        compiler_params=pltpu.CompilerParams(vmem_limit_bytes=60 * MIB),
        name="pick",
    )(place, query_weight, key_weight, value_weight, out_weight)


def normalize_kernel(shift_ref, gain_ref, rows_ref, out_ref):
    for step in range(2):
        floats = rows_ref[step].astype(F32)
        centered = floats - jnp.mean(floats, axis=-1, keepdims=True)
        variance = jnp.mean(centered * centered, axis=-1, keepdims=True)
        normed = centered * lax.rsqrt(variance + EPS)
        out_ref[step] = (normed * gain_ref[step : step + 1] + shift_ref[step : step + 1]).astype(
            BF16
        )


def normalize(shift, gain, rows):
    return pl.pallas_call(
        normalize_kernel,
        out_shape=jax.ShapeDtypeStruct(rows.shape, BF16),
        in_specs=[VMEM] * 3,
        out_specs=VMEM,
        compiler_params=pltpu.CompilerParams(vmem_limit_bytes=24 * MIB),
        cost_estimate=pl.CostEstimate(
            flops=16 * rows.size, bytes_accessed=8 * rows.size, transcendentals=0
        ),
        name="normalize",
    )(shift, gain, rows)


def tile_kernel(place_ref, *refs):
    sources, tile_ref = refs[:-1], refs[-1]
    low, pair = tile_ref.shape[2], sources[0].shape[-1]
    for k, ref in enumerate(sources):
        for half in range(2):
            tile_ref[:, place_ref[1 + k], :, half * pair : (half + 1) * pair] = ref[
                :, half * low : (half + 1) * low
            ]


def tile_of(place, sources):
    depth, height, pair = sources[0].shape
    across = len(sources)
    return pl.pallas_call(
        tile_kernel,
        out_shape=jax.ShapeDtypeStruct((depth, across, height // 2, 2 * pair), BF16),
        in_specs=[SMEM] + [VMEM] * across,
        out_specs=VMEM,
        compiler_params=pltpu.CompilerParams(vmem_limit_bytes=60 * MIB),
        name="tile",
    )(place, *sources).reshape(-1, 2 * pair)


def attend_kernel(place_ref, sizes_ref, source_ref, *refs):
    blocks, outs = refs[:10], refs[10:14]
    (
        sums_ref,
        parts_ref,
        keys_ref,
        values_ref,
        block_ref,
        order_ref,
        rows_ref,
        weight_ref,
        sems,
        weight_sems,
    ) = refs[14:]
    steps, groups, rows, width = rows_ref.shape
    pair = 2 * HEAD_DIM
    half = rows // 2

    fetches = [
        pltpu.make_async_copy(source_ref.at[x], weight_ref.at[:, x], weight_sems.at[x])
        for x in range(source_ref.shape[0])
    ]
    units = []
    for step in range(steps):
        for group in range(groups):
            pairs = []
            for side in range(2):
                if group < 3:
                    source = blocks[2 * group + side].at[step]
                else:
                    source = blocks[6 + 2 * side + step].at[0]
                pairs.append(
                    pltpu.make_async_copy(
                        source,
                        rows_ref.at[step, group, pl.ds(side * half, half)],
                        sems.at[step, group, side],
                    )
                )
            units.append(pairs)

    def start(unit):
        for load in units[unit] if unit < len(units) else []:
            load.start()

    for fetch in fetches:
        fetch.start()
    for unit in range(2):
        start(unit)
    values_ref[:, pair:] = jnp.ones((groups * rows, pair), BF16)
    for fetch in fetches:
        fetch.wait()
    for unit in range(2, 4):
        start(unit)

    weight = weight_ref.reshape(width, weight_ref.shape[-1])
    first = lax.broadcasted_iota(jnp.int32, (1, pair), 1) < HEAD_DIM
    scale = HEAD_DIM ** (-0.5)
    for step in range(steps):
        for group in range(groups):
            unit = step * groups + group
            for load in units[unit]:
                load.wait()
            start(unit + 4)
            part = jnp.dot(
                rows_ref[step, group], weight[...], preferred_element_type=F32
            ).astype(BF16)
            span = slice(group * rows, (group + 1) * rows)
            parts_ref[span, :] = part[:, :pair]
            keys_ref[span, :] = part[:, pair : 2 * pair]
            values_ref[span, :pair] = part[:, 2 * pair :]
        for position in range(groups):
            queries = parts_ref[position * rows : (position + 1) * rows, :].astype(F32) * scale
            heads = []
            for mask in (first, jnp.logical_not(first)):
                chosen = jnp.where(mask, queries, 0.0).astype(BF16)
                scores = lax.dot_general(
                    chosen, keys_ref[...], (((1,), (1,)), ((), ())), preferred_element_type=F32
                )
                weights = jnp.exp(scores - jnp.max(scores, axis=-1, keepdims=True)).astype(BF16)
                summed = jnp.dot(weights, values_ref[...], preferred_element_type=F32)
                heads.append(summed[:, :pair] / summed[:, pair:])
            attended = jnp.where(first, heads[0], heads[1]).astype(BF16)
            for side in range(2):
                block = attended[side * half : (side + 1) * half]
                spot = place_ref[5 + 2 * position + side]
                outs[position][side, step] = block
                scaled = sizes_ref[step] * block.astype(F32)
                if step == 0:
                    block_ref[spot] = scaled
                else:
                    block_ref[spot] = block_ref[spot] + scaled
    targets, depth = sums_ref.shape[:2]
    per = half // targets
    for field in range(block_ref.shape[0]):
        for turn in range(per):
            order_ref[pl.ds(per * field + turn, targets, stride=depth), :] = block_ref[
                field, turn * targets : (turn + 1) * targets
            ]
    sums_ref[...] = order_ref[...].astype(BF16).reshape(sums_ref.shape)


def attend(place, sizes, weights, blocks, targets):
    steps, half, width = blocks[0].shape
    across, depth, height, columns = weights.shape
    pair = columns // 3
    groups, rows = 4, 2 * half
    length = groups * rows
    block = jax.ShapeDtypeStruct((2, steps, half, pair), BF16)
    *outs, sums = pl.pallas_call(
        attend_kernel,
        out_shape=(block,) * groups
        + (jax.ShapeDtypeStruct((targets, length // targets, pair), BF16),),
        in_specs=[SMEM] * 2 + [HBM] * (1 + len(blocks)),
        out_specs=(VMEM,) * (groups + 1),
        scratch_shapes=[
            pltpu.VMEM((length, pair), BF16),
            pltpu.VMEM((length, pair), BF16),
            pltpu.VMEM((length, 2 * pair), BF16),
            pltpu.VMEM((2 * groups, half, pair), F32),
            pltpu.VMEM((length, pair), F32),
            pltpu.VMEM((steps, groups, rows, width), BF16),
            pltpu.VMEM((depth, across, height, columns), BF16),
            pltpu.SemaphoreType.DMA((steps, groups, 2)),
            pltpu.SemaphoreType.DMA((across,)),
        ],
        compiler_params=pltpu.CompilerParams(vmem_limit_bytes=60 * MIB),
        cost_estimate=pl.CostEstimate(
            flops=16 * length * length * pair + 12 * length * width * pair,
            bytes_accessed=4 * length * width + 8 * width * pair,
            transcendentals=4 * length * length,
        ),
        name="attend",
    )(place, sizes, weights, *blocks)
    return outs, sums


def earlier_kernel(sums_ref, out_ref):
    running = jnp.zeros(sums_ref.shape[1:], F32)
    for index in range(sums_ref.shape[0]):
        out_ref[index] = running.astype(BF16)
        running = running + sums_ref[index].astype(F32)


def earlier(sums):
    return pl.pallas_call(
        earlier_kernel,
        out_shape=jax.ShapeDtypeStruct(sums.shape, BF16),
        in_specs=[VMEM],
        out_specs=VMEM,
        compiler_params=pltpu.CompilerParams(vmem_limit_bytes=16 * MIB),
        name="earlier",
    )(sums)


def total_kernel(place_ref, sizes_ref, before_ref, initial_ref, *refs):
    blocks, tiles = refs[:8], refs[8:16]
    out_ref, order_ref, rows_ref, weight_ref, result_ref, load_sems, store_sems = refs[16:]
    groups, depth, pair = before_ref.shape
    rows = initial_ref.shape[0]
    per = rows // groups
    width = weight_ref.shape[-1]
    loads = [
        pltpu.make_async_copy(source, weight_ref.at[index], load_sems.at[index])
        for index, source in enumerate(tiles)
    ]
    for load in loads:
        load.start()

    order_ref[...] = before_ref[...].astype(F32).reshape(order_ref.shape)
    for field in range(depth // per):
        columns = slice(field * pair, (field + 1) * pair)
        for turn in range(per):
            rows_ref[turn * groups : (turn + 1) * groups, columns] = order_ref[
                pl.ds(per * field + turn, groups, stride=depth), :
            ].astype(BF16)
    for index, ref in enumerate(blocks):
        start = pl.multiple_of(place_ref[21 + index] * pair, pair)
        for step in range(2):
            rows_ref[(1 + step) * rows : (2 + step) * rows, pl.ds(start, pair)] = ref[
                index // 4, step
            ]

    for load in loads:
        load.wait()
    stores = []
    for index in range(len(loads)):
        start = pl.multiple_of(place_ref[13 + index] * width, width)
        drift = jnp.dot(rows_ref[...], weight_ref[index], preferred_element_type=F32)
        base = (
            initial_ref[:, pl.ds(start, width)].astype(F32)
            + drift[:rows]
            + sizes_ref[0] * drift[rows : 2 * rows]
        )
        result_ref[index, 0] = base
        result_ref[index, 1] = base + sizes_ref[1] * drift[2 * rows :]
        store = pltpu.make_async_copy(
            result_ref.at[index], out_ref.at[:, :, pl.ds(start, width)], store_sems.at[index]
        )
        store.start()
        stores.append(store)
    for store in stores:
        store.wait()


def totals(place, sizes, before, initial, blocks, tiles):
    rows, width = initial.shape
    groups, depth, pair = before.shape
    count = len(tiles)
    return pl.pallas_call(
        total_kernel,
        out_shape=jax.ShapeDtypeStruct((2, rows, width), F32),
        in_specs=[SMEM] * 2 + [VMEM] * 10 + [HBM] * 8,
        out_specs=HBM,
        scratch_shapes=[
            pltpu.VMEM((groups * depth, pair), F32),
            pltpu.VMEM((3 * rows, tiles[0].shape[0]), BF16),
            pltpu.VMEM((count,) + tiles[0].shape, BF16),
            pltpu.VMEM((count, 2, rows, tiles[0].shape[1]), F32),
            pltpu.SemaphoreType.DMA((count,)),
            pltpu.SemaphoreType.DMA((count,)),
        ],
        compiler_params=pltpu.CompilerParams(vmem_limit_bytes=60 * MIB),
        name="totals",
    )(place, sizes, before, initial, *blocks, *tiles)


def gather_depth(blocks, shape):
    return lax.all_to_all(
        blocks,
        "step",
        0,
        0,
        axis_index_groups=[[x + shape[1] * z for z in range(shape[0])] for x in range(shape[1])],
    )


def fetch_column(block, shape, by):
    across = shape[1]
    return lax.ppermute(
        block,
        "step",
        [(i, i // across * across + (i - by) % across) for i in range(shape[0] * across)],
    )


def gather_columns(block, shape):
    across = shape[1]
    return lax.all_to_all(
        jnp.broadcast_to(block[None], (across,) + block.shape),
        "step",
        0,
        0,
        axis_index_groups=[[z * across + x for x in range(across)] for z in range(shape[0])],
    )


def local(
    trajectory,
    initial,
    step_sizes,
    time_index,
    plan,
    adaln_weight,
    query_weight,
    key_weight,
    value_weight,
    out_weight,
):
    fields = lax.axis_size("seq")
    groups = lax.axis_size("step")
    chips = fields // 2
    shape = (groups // 4, 4)
    place = lax.axis_index("seq")
    chip, core = place // 2, place % 2
    pair = 2 * HEAD_DIM
    swap = [(i, i ^ 1) for i in range(fields)]

    def along_ring(block, by):
        return lax.ppermute(block, "seq", [(i, (i + 2 * by) % fields) for i in range(fields)])

    shifts_by = (1, chips - 1, 2)
    column = lax.axis_index("step") % 4
    source_chips = [chip] + [(chip - by) % chips for by in shifts_by]
    head_chips = [chip] + [(chip + by) % chips for by in shifts_by]
    index = jnp.stack(
        [place]
        + [(column + by) % 4 for by in range(4)]
        + [spot for source in source_chips for spot in (2 * source + core, 2 * source + 1 - core)]
        + [2 * source + core for source in source_chips]
        + [2 * source + 1 - core for source in source_chips]
        + [2 * source + core for source in head_chips]
        + [2 * source + 1 - core for source in head_chips]
    ).astype(jnp.int32)

    picked = pick(
        index,
        query_weight,
        key_weight,
        value_weight,
        out_weight,
        shape[0],
    )
    along = gather_depth(picked, shape)
    weights = gather_columns(along[:, :, : 3 * pair], shape)
    out_along = along[:, :, 3 * pair :]
    out_blocks = [out_along] + [fetch_column(out_along, shape, by) for by in range(1, shape[1])]
    out_tile = tile_of(index, out_blocks)

    shifts, scales = modulation(time_index, plan, adaln_weight)
    gains = 1.0 + scales

    def partner_of(block):
        return lax.ppermute(block, "seq", swap)

    here = normalize(shifts, gains, trajectory)
    behind, ahead = along_ring(here, 1), along_ring(here, chips - 1)
    opposite = [along_ring(behind[:1], 1), along_ring(ahead[1:], chips - 1)]
    blocks = []
    for block in (here, behind, ahead):
        blocks += [block, partner_of(block)]
    opposite, out_tile = lax.optimization_barrier((opposite, out_tile))
    blocks += opposite + [partner_of(block) for block in opposite]
    out_tiles = [out_tile] + [along_ring(out_tile, by) for by in shifts_by]
    attended, sums = attend(index, step_sizes, weights, blocks, groups)
    out_tiles, _ = lax.optimization_barrier((out_tiles, sums))
    out_tiles = out_tiles + [partner_of(tile) for tile in out_tiles]

    per = sums.shape[1] // fields
    received = lax.all_to_all(
        sums.reshape(groups * fields, per, pair), ("step", "seq"), 0, 0
    ).reshape(sums.shape)
    before = lax.all_to_all(earlier(received), "step", 0, 0)

    arrived = [attended[0]] + [
        along_ring(block, chips - by) for block, by in zip(attended[1:], shifts_by)
    ]
    arrived = arrived + [partner_of(block) for block in arrived]
    return totals(index, step_sizes, before, initial, arrived, out_tiles)


def solution(mesh):
    in_specs = (
        P("step", "seq", None),
        P("seq", None),
        P("step"),
        P("step"),
        P(),
        P(),
        P("step", None),
        P("step", None),
        P("step", None),
        P("step", None),
    )
    out_specs = P("step", "seq", None)
    return jax.shard_map(local, mesh=mesh, in_specs=in_specs, out_specs=out_specs, check_vma=False)
```

```python
import functools

import jax
import jax.numpy as jnp
from jax import lax
from jax.experimental import pallas as pl
from jax.experimental.pallas import tpu as pltpu
from jax.sharding import PartitionSpec as P

HEAD_DIM = 64
EPS = 1e-06
BF16 = jnp.bfloat16
F32 = jnp.float32
MIB = 1024 * 1024
VMEM = pl.BlockSpec(memory_space=pltpu.VMEM)
SMEM = pl.BlockSpec(memory_space=pltpu.SMEM)
HBM = pl.BlockSpec(memory_space=pl.ANY)


def modulation(time_index, plan, adaln_weight):
    table_size = plan.shape[0]
    onehot = (time_index[:, None] == jnp.arange(table_size, dtype=jnp.int32)[None, :]).astype(F32)
    sigmas = jnp.sum(onehot * plan[None, :], axis=1)
    half_width = adaln_weight.shape[0] // 2
    frequency = 0.25 * jnp.exp(4.0 * jnp.arange(half_width, dtype=F32) / half_width)
    angles = jnp.log(sigmas)[:, None] * frequency[None, :]
    embedding = jnp.concatenate([jnp.cos(angles), jnp.sin(angles)], axis=1).astype(BF16)
    modulated = jnp.dot(embedding, adaln_weight, preferred_element_type=F32)
    feature_width = adaln_weight.shape[1] // 2
    return (modulated[:, :feature_width], modulated[:, feature_width:])


def pick_kernel(place_ref, query_ref, key_ref, value_ref, out_weight_ref, picked_ref):
    pair = picked_ref.shape[-1] // 4
    column = pl.multiple_of(place_ref[0] * pair, pair)
    blocks = [ref[:, pl.ds(column, pair)] for ref in (query_ref, key_ref, value_ref)]
    halves = []
    for half in range(2):
        start = pl.multiple_of((2 * place_ref[0] + half) * pair, pair)
        halves.append(out_weight_ref[:, pl.ds(start, pair)])
    picked = jnp.concatenate(blocks + [jnp.concatenate(halves, axis=0)], axis=1)
    for copy in range(picked_ref.shape[0]):
        picked_ref[copy] = picked


def pick(place, query_weight, key_weight, value_weight, out_weight, copies):
    rows = query_weight.shape[0]
    return pl.pallas_call(
        pick_kernel,
        out_shape=jax.ShapeDtypeStruct((copies, rows, 8 * HEAD_DIM), BF16),
        in_specs=[SMEM] + [VMEM] * 4,
        out_specs=VMEM,
        compiler_params=pltpu.CompilerParams(vmem_limit_bytes=60 * MIB),
        name="pick",
    )(place, query_weight, key_weight, value_weight, out_weight)


def normalize_kernel(shift_ref, gain_ref, rows_ref, out_ref):
    for step in range(2):
        floats = rows_ref[step].astype(F32)
        centered = floats - jnp.mean(floats, axis=-1, keepdims=True)
        variance = jnp.mean(centered * centered, axis=-1, keepdims=True)
        normed = centered * lax.rsqrt(variance + EPS)
        out_ref[step] = (normed * gain_ref[step : step + 1] + shift_ref[step : step + 1]).astype(
            BF16
        )


def normalize(shift, gain, rows):
    return pl.pallas_call(
        normalize_kernel,
        out_shape=jax.ShapeDtypeStruct(rows.shape, BF16),
        in_specs=[VMEM] * 3,
        out_specs=VMEM,
        compiler_params=pltpu.CompilerParams(vmem_limit_bytes=24 * MIB),
        cost_estimate=pl.CostEstimate(
            flops=16 * rows.size, bytes_accessed=8 * rows.size, transcendentals=0
        ),
        name="normalize",
    )(shift, gain, rows)


def tile_kernel(place_ref, *refs):
    sources, tile_ref = refs[:-1], refs[-1]
    low, pair = tile_ref.shape[2], sources[0].shape[-1]
    for k, ref in enumerate(sources):
        for half in range(2):
            tile_ref[:, place_ref[1 + k], :, half * pair : (half + 1) * pair] = ref[
                :, half * low : (half + 1) * low
            ]


def tile_of(place, sources):
    depth, height, pair = sources[0].shape
    across = len(sources)
    return pl.pallas_call(
        tile_kernel,
        out_shape=jax.ShapeDtypeStruct((depth, across, height // 2, 2 * pair), BF16),
        in_specs=[SMEM] + [VMEM] * across,
        out_specs=VMEM,
        compiler_params=pltpu.CompilerParams(vmem_limit_bytes=60 * MIB),
        name="tile",
    )(place, *sources).reshape(-1, 2 * pair)


def attend_kernel(place_ref, sizes_ref, source_ref, *refs):
    blocks, outs = refs[:10], refs[10:14]
    (
        sums_ref,
        parts_ref,
        keys_ref,
        values_ref,
        block_ref,
        order_ref,
        rows_ref,
        weight_ref,
        sems,
        weight_sems,
    ) = refs[14:]
    steps, groups, rows, width = rows_ref.shape
    pair = 2 * HEAD_DIM
    half = rows // 2

    fetches = [
        pltpu.make_async_copy(source_ref.at[x], weight_ref.at[:, x], weight_sems.at[x])
        for x in range(source_ref.shape[0])
    ]
    units = []
    for step in range(steps):
        for group in range(groups):
            pairs = []
            for side in range(2):
                if group < 3:
                    source = blocks[2 * group + side].at[step]
                else:
                    source = blocks[6 + 2 * side + step].at[0]
                pairs.append(
                    pltpu.make_async_copy(
                        source,
                        rows_ref.at[step, group, pl.ds(side * half, half)],
                        sems.at[step, group, side],
                    )
                )
            units.append(pairs)

    def start(unit):
        for load in units[unit] if unit < len(units) else []:
            load.start()

    for fetch in fetches:
        fetch.start()
    for unit in range(2):
        start(unit)
    values_ref[:, pair:] = jnp.ones((groups * rows, pair), BF16)
    for fetch in fetches:
        fetch.wait()
    for unit in range(2, 4):
        start(unit)

    weight = weight_ref.reshape(width, weight_ref.shape[-1])
    first = lax.broadcasted_iota(jnp.int32, (1, pair), 1) < HEAD_DIM
    scale = HEAD_DIM ** (-0.5)
    for step in range(steps):
        for group in range(groups):
            unit = step * groups + group
            for load in units[unit]:
                load.wait()
            start(unit + 4)
            part = jnp.dot(
                rows_ref[step, group], weight[...], preferred_element_type=F32
            ).astype(BF16)
            span = slice(group * rows, (group + 1) * rows)
            parts_ref[span, :] = part[:, :pair]
            keys_ref[span, :] = part[:, pair : 2 * pair]
            values_ref[span, :pair] = part[:, 2 * pair :]
        for position in range(groups):
            queries = parts_ref[position * rows : (position + 1) * rows, :].astype(F32) * scale
            heads = []
            for mask in (first, jnp.logical_not(first)):
                chosen = jnp.where(mask, queries, 0.0).astype(BF16)
                scores = lax.dot_general(
                    chosen, keys_ref[...], (((1,), (1,)), ((), ())), preferred_element_type=F32
                )
                weights = jnp.exp(scores - jnp.max(scores, axis=-1, keepdims=True)).astype(BF16)
                summed = jnp.dot(weights, values_ref[...], preferred_element_type=F32)
                heads.append(summed[:, :pair] / summed[:, pair:])
            attended = jnp.where(first, heads[0], heads[1]).astype(BF16)
            for side in range(2):
                block = attended[side * half : (side + 1) * half]
                spot = place_ref[5 + 2 * position + side]
                outs[position][side, step] = block
                scaled = sizes_ref[step] * block.astype(F32)
                if step == 0:
                    block_ref[spot] = scaled
                else:
                    block_ref[spot] = block_ref[spot] + scaled
    targets, depth = sums_ref.shape[:2]
    per = half // targets
    for field in range(block_ref.shape[0]):
        for turn in range(per):
            order_ref[pl.ds(per * field + turn, targets, stride=depth), :] = block_ref[
                field, turn * targets : (turn + 1) * targets
            ]
    sums_ref[...] = order_ref[...].astype(BF16).reshape(sums_ref.shape)


def attend(place, sizes, weights, blocks, targets):
    steps, half, width = blocks[0].shape
    across, depth, height, columns = weights.shape
    pair = columns // 3
    groups, rows = 4, 2 * half
    length = groups * rows
    block = jax.ShapeDtypeStruct((2, steps, half, pair), BF16)
    *outs, sums = pl.pallas_call(
        attend_kernel,
        out_shape=(block,) * groups
        + (jax.ShapeDtypeStruct((targets, length // targets, pair), BF16),),
        in_specs=[SMEM] * 2 + [HBM] * (1 + len(blocks)),
        out_specs=(VMEM,) * (groups + 1),
        scratch_shapes=[
            pltpu.VMEM((length, pair), BF16),
            pltpu.VMEM((length, pair), BF16),
            pltpu.VMEM((length, 2 * pair), BF16),
            pltpu.VMEM((2 * groups, half, pair), F32),
            pltpu.VMEM((length, pair), F32),
            pltpu.VMEM((steps, groups, rows, width), BF16),
            pltpu.VMEM((depth, across, height, columns), BF16),
            pltpu.SemaphoreType.DMA((steps, groups, 2)),
            pltpu.SemaphoreType.DMA((across,)),
        ],
        compiler_params=pltpu.CompilerParams(vmem_limit_bytes=60 * MIB),
        cost_estimate=pl.CostEstimate(
            flops=16 * length * length * pair + 12 * length * width * pair,
            bytes_accessed=4 * length * width + 8 * width * pair,
            transcendentals=4 * length * length,
        ),
        name="attend",
    )(place, sizes, weights, *blocks)
    return outs, sums


def earlier_kernel(sums_ref, out_ref):
    running = jnp.zeros(sums_ref.shape[1:], F32)
    for index in range(sums_ref.shape[0]):
        out_ref[index] = running.astype(BF16)
        running = running + sums_ref[index].astype(F32)


def earlier(sums):
    return pl.pallas_call(
        earlier_kernel,
        out_shape=jax.ShapeDtypeStruct(sums.shape, BF16),
        in_specs=[VMEM],
        out_specs=VMEM,
        compiler_params=pltpu.CompilerParams(vmem_limit_bytes=16 * MIB),
        name="earlier",
    )(sums)


def total_kernel(place_ref, sizes_ref, before_ref, initial_ref, *refs):
    blocks, tiles = refs[:8], refs[8:16]
    out_ref, order_ref, rows_ref, weight_ref, result_ref, load_sems, store_sems = refs[16:]
    groups, depth, pair = before_ref.shape
    rows = initial_ref.shape[0]
    per = rows // groups
    width = weight_ref.shape[-1]
    loads = [
        pltpu.make_async_copy(source, weight_ref.at[index], load_sems.at[index])
        for index, source in enumerate(tiles)
    ]
    for load in loads:
        load.start()

    order_ref[...] = before_ref[...].astype(F32).reshape(order_ref.shape)
    for field in range(depth // per):
        columns = slice(field * pair, (field + 1) * pair)
        for turn in range(per):
            rows_ref[turn * groups : (turn + 1) * groups, columns] = order_ref[
                pl.ds(per * field + turn, groups, stride=depth), :
            ].astype(BF16)
    for index, ref in enumerate(blocks):
        start = pl.multiple_of(place_ref[21 + index] * pair, pair)
        for step in range(2):
            rows_ref[(1 + step) * rows : (2 + step) * rows, pl.ds(start, pair)] = ref[
                index // 4, step
            ]

    for load in loads:
        load.wait()
    stores = []
    for index in range(len(loads)):
        start = pl.multiple_of(place_ref[13 + index] * width, width)
        drift = jnp.dot(rows_ref[...], weight_ref[index], preferred_element_type=F32)
        base = (
            initial_ref[:, pl.ds(start, width)].astype(F32)
            + drift[:rows]
            + sizes_ref[0] * drift[rows : 2 * rows]
        )
        result_ref[index, 0] = base
        result_ref[index, 1] = base + sizes_ref[1] * drift[2 * rows :]
        store = pltpu.make_async_copy(
            result_ref.at[index], out_ref.at[:, :, pl.ds(start, width)], store_sems.at[index]
        )
        store.start()
        stores.append(store)
    for store in stores:
        store.wait()


def totals(place, sizes, before, initial, blocks, tiles):
    rows, width = initial.shape
    groups, depth, pair = before.shape
    count = len(tiles)
    return pl.pallas_call(
        total_kernel,
        out_shape=jax.ShapeDtypeStruct((2, rows, width), F32),
        in_specs=[SMEM] * 2 + [VMEM] * 10 + [HBM] * 8,
        out_specs=HBM,
        scratch_shapes=[
            pltpu.VMEM((groups * depth, pair), F32),
            pltpu.VMEM((3 * rows, tiles[0].shape[0]), BF16),
            pltpu.VMEM((count,) + tiles[0].shape, BF16),
            pltpu.VMEM((count, 2, rows, tiles[0].shape[1]), F32),
            pltpu.SemaphoreType.DMA((count,)),
            pltpu.SemaphoreType.DMA((count,)),
        ],
        compiler_params=pltpu.CompilerParams(vmem_limit_bytes=60 * MIB),
        name="totals",
    )(place, sizes, before, initial, *blocks, *tiles)


def gather_depth(blocks, shape):
    return lax.all_to_all(
        blocks,
        "step",
        0,
        0,
        axis_index_groups=[[x + shape[1] * z for z in range(shape[0])] for x in range(shape[1])],
    )


def fetch_column(block, shape, by):
    across = shape[1]
    return lax.ppermute(
        block,
        "step",
        [(i, i // across * across + (i - by) % across) for i in range(shape[0] * across)],
    )


def gather_columns(block, shape):
    across = shape[1]
    return lax.all_to_all(
        jnp.broadcast_to(block[None], (across,) + block.shape),
        "step",
        0,
        0,
        axis_index_groups=[[z * across + x for x in range(across)] for z in range(shape[0])],
    )


def local(
    trajectory,
    initial,
    step_sizes,
    time_index,
    plan,
    adaln_weight,
    query_weight,
    key_weight,
    value_weight,
    out_weight,
):
    fields = lax.axis_size("seq")
    groups = lax.axis_size("step")
    chips = fields // 2
    shape = (groups // 4, 4)
    place = lax.axis_index("seq")
    chip, core = place // 2, place % 2
    pair = 2 * HEAD_DIM
    swap = [(i, i ^ 1) for i in range(fields)]

    def along_ring(block, by):
        return lax.ppermute(block, "seq", [(i, (i + 2 * by) % fields) for i in range(fields)])

    shifts_by = (1, chips - 1, 2)
    column = lax.axis_index("step") % 4
    source_chips = [chip] + [(chip - by) % chips for by in shifts_by]
    head_chips = [chip] + [(chip + by) % chips for by in shifts_by]
    index = jnp.stack(
        [place]
        + [(column + by) % 4 for by in range(4)]
        + [spot for source in source_chips for spot in (2 * source + core, 2 * source + 1 - core)]
        + [2 * source + core for source in source_chips]
        + [2 * source + 1 - core for source in source_chips]
        + [2 * source + core for source in head_chips]
        + [2 * source + 1 - core for source in head_chips]
    ).astype(jnp.int32)

    picked = pick(
        index,
        query_weight,
        key_weight,
        value_weight,
        out_weight,
        shape[0],
    )
    along = gather_depth(picked, shape)
    weights = gather_columns(along[:, :, : 3 * pair], shape)
    out_along = along[:, :, 3 * pair :]
    out_blocks = [out_along] + [fetch_column(out_along, shape, by) for by in range(1, shape[1])]
    out_tile = tile_of(index, out_blocks)

    shifts, scales = modulation(time_index, plan, adaln_weight)
    gains = 1.0 + scales

    def partner_of(block):
        return lax.ppermute(block, "seq", swap)

    here = normalize(shifts, gains, trajectory)
    behind, ahead = along_ring(here, 1), along_ring(here, chips - 1)
    opposite = [along_ring(behind[:1], 1), along_ring(ahead[1:], chips - 1)]
    blocks = []
    for block in (here, behind, ahead):
        blocks += [block, partner_of(block)]
    opposite, out_tile = lax.optimization_barrier((opposite, out_tile))
    blocks += opposite + [partner_of(block) for block in opposite]
    out_tiles = [out_tile] + [along_ring(out_tile, by) for by in shifts_by[:2]]
    attended, sums = attend(index, step_sizes, weights, blocks, groups)
    out_tiles, _ = lax.optimization_barrier((out_tiles, sums))
    out_tiles = out_tiles + [along_ring(out_tiles[1], 1)]
    out_tiles = out_tiles + [partner_of(tile) for tile in out_tiles]

    per = sums.shape[1] // fields
    received = lax.all_to_all(
        sums.reshape(groups * fields, per, pair), ("step", "seq"), 0, 0
    ).reshape(sums.shape)
    before = lax.all_to_all(earlier(received), "step", 0, 0)

    arrived = [attended[0]] + [
        along_ring(block, chips - by) for block, by in zip(attended[1:], shifts_by)
    ]
    arrived = arrived + [partner_of(block) for block in arrived]
    return totals(index, step_sizes, before, initial, arrived, out_tiles)


def solution(mesh):
    in_specs = (
        P("step", "seq", None),
        P("seq", None),
        P("step"),
        P("step"),
        P(),
        P(),
        P("step", None),
        P("step", None),
        P("step", None),
        P("step", None),
    )
    out_specs = P("step", "seq", None)
    return jax.shard_map(local, mesh=mesh, in_specs=in_specs, out_specs=out_specs, check_vma=False)
```
